256 devices in a mesh: rep: 16 (over y, z_lo, core), fsdp: 16 (over z_hi, x).
Axes of the slice: x: 4, y: 4, z: 8 (z_hi: 4, z_lo: 2; z = z_hi * 2 + z_lo), core: 2. Of those that a mesh axis runs over, the one named last changes fastest.
Arguments:
- tokens: bfloat16 [65536, 6144], P(('rep', 'fsdp')), may hold values from -6 to 6
- targets: bfloat16 [65536, 1024], P(('rep', 'fsdp')), may hold values from -6 to 6
- weight: bfloat16 [16, 6144, 1024], P('rep', 'fsdp'), may hold values from -6 to 6
- moment_first: float32 [16, 6144, 1024], P('rep', 'fsdp'), may hold values from -6 to 6
- moment_second: float32 [16, 6144, 1024], P('rep', 'fsdp'), may hold values from 0.5 to 4
- fragment_local: bfloat16 [16, 6144, 1024], P('rep', 'fsdp'), may hold values from -6 to 6
- global_params: float32 [2, 6144, 1024], P(None, 'fsdp', 'rep'), may hold values from -6 to 6
- outer_moment: float32 [2, 6144, 1024], P(None, 'fsdp', 'rep'), may hold values from -4 to 4
- fragment: int32 [1], replicated, may hold values from 0 to 1
Outputs:
- new_weight: bfloat16 [16, 6144, 1024], P('rep', 'fsdp')
- new_first: float32 [16, 6144, 1024], P('rep', 'fsdp')
- new_second: float32 [16, 6144, 1024], P('rep', 'fsdp')
- new_fragment: bfloat16 [16, 6144, 1024], P('rep', 'fsdp')
- new_global: float32 [2, 6144, 1024], P(None, 'fsdp', 'rep')
- new_outer: float32 [2, 6144, 1024], P(None, 'fsdp', 'rep')
The draws below stay inside these ranges and needn't reach their ends.
All inputs are finite; a program needn't handle non-finite values.
Results may differ from the reference program's by a relative error of at most 0.013.
Values may be sent and summed in bfloat16 or wider, within the bound.
No kernel may reach another device: no remote copies, remote signals or barrier semaphores. Data moves between devices by JAX's collectives and lax.ppermute only.
A program may use at most 128 MiB of HBM per device.

```python
import math
import jax
import jax.numpy as jnp
from jax import lax

D = 6144
KV = 1024
TOK_DEV = 256
FRAGS = 2
TOKENS = 65536
N_REP = 16
N_FSDP = 16


def spiked(drawn, own_key, source, target, parts, factor):
    owner, partner = [(jnp.arange(drawn.shape[axis_at]) // (drawn.shape[axis_at] // parts)).reshape([-1 if axis == axis_at else 1 for axis in range(drawn.ndim)]) for axis_at in (source, target)]
    chosen = jax.random.permutation(own_key, parts)[partner]
    strong = (owner == chosen) | (owner == (partner + parts // 2) % parts)
    return jnp.where(strong, factor * drawn, drawn)


def steps_of(key, extent, shards, least, high):
    def one(position, parts):
        heights = jax.random.uniform(jax.random.fold_in(jax.random.fold_in(key, 6), position), (parts,), jnp.float32, least / len(shards), high / len(shards))
        return jnp.repeat(jnp.exp(heights), extent[position] // parts).reshape((-1,) + (1,) * (len(extent) - position - 1))

    level = one(*shards[0])
    for cut in shards[1:]:
        level = level * one(*cut)
    return level


def bell_draw(stream_key, shape, width, reach, shards=(), kind=jnp.bfloat16):
    entries = width * jax.random.normal(stream_key, shape, jnp.float32)
    if shards:
        entries = entries * steps_of(stream_key, shape, shards, -0.22, 0.18)
    return jnp.clip(entries, -reach, reach).astype(kind)


def gaussian_with(rng, shape, spread, bound, pieces, heavy, held_as=jnp.bfloat16):
    values = spread * jax.random.normal(rng, shape, jnp.float32)
    if pieces:
        values = values * steps_of(rng, shape, pieces, -0.22, 0.18)
    return jnp.clip(spiked(values, jax.random.fold_in(rng, 3), *heavy), -bound, bound).astype(held_as)


def setup_inputs(seed: int = 0) -> dict:
    splits = jax.random.split(jax.random.key(seed), 10)
    tokens = bell_draw(splits[0], (TOKENS, D), 1.0, 6.0, ((0, 256),))
    targets = bell_draw(splits[1], (TOKENS, KV), 1.0, 6.0, ((0, 256),))
    weight = bell_draw(splits[2], (N_REP, D, KV), 1.0, 6.0, ((0, 16), (1, 16)))
    moment_first = bell_draw(splits[3], (N_REP, D, KV), 1.0, 6.0, ((0, 16), (1, 16)), jnp.float32)
    moment_second = jnp.clip(jnp.exp(math.log(4.0) - 2.0794415 * jax.random.uniform(splits[4], (N_REP, D, KV), jnp.float32) ** steps_of(splits[4], (N_REP, D, KV), ((0, 16), (1, 16)), -0.2, 0.2)), 0.5, 4.0)
    fragment_local = gaussian_with(splits[5], (N_REP, D, KV), 1.0, 6.0, ((0, 16), (1, 16)), (0, 2, 16, 2.0))
    global_params = bell_draw(splits[6], (FRAGS, D, KV), 1.0, 6.0, ((1, 16), (2, 16)), jnp.float32)
    outer_moment = bell_draw(splits[7], (FRAGS, D, KV), 0.5, 4.0, ((1, 16), (2, 16)), jnp.float32)
    fragment = jax.random.randint(splits[8], (1,), 0, FRAGS).astype(jnp.int32)
    return dict(tokens=tokens, targets=targets, weight=weight, moment_first=moment_first, moment_second=moment_second, fragment_local=fragment_local, global_params=global_params, outer_moment=outer_moment, fragment=fragment)


def inner_step(rows, goals, weight, first, second):
    inv_root = 1.0 / jnp.sqrt(jnp.float32(D))
    scale = 1.0 / jnp.sqrt(jnp.float32(TOK_DEV * N_FSDP))
    keys = jnp.dot(rows, weight, preferred_element_type=jnp.float32) * inv_root
    resid = (keys - goals.astype(jnp.float32)).astype(jnp.bfloat16)
    grad = lax.dot_general(rows, resid, (((0,), (0,)), ((), ())), preferred_element_type=jnp.float32) * scale
    new_first = 0.9 * first + 0.1 * grad
    new_second = 0.95 * second + 0.05 * grad * grad
    wide = weight.astype(jnp.float32)
    new_weight = (wide - 0.3 * (new_first / (jnp.sqrt(new_second) + 1e-08) + 0.1 * wide)).astype(jnp.bfloat16)
    return (new_weight, new_first, new_second)

def reference(tokens, targets, weight, moment_first, moment_second, fragment_local, global_params, outer_moment, fragment):
    per = TOK_DEV * N_FSDP
    rows = tokens.reshape(N_REP, per, D)
    goals = targets.reshape(N_REP, per, KV)
    new_weight, new_first, new_second = lax.map(lambda a: inner_step(*a), (rows, goals, weight, moment_first, moment_second))
    index = fragment[0].astype(jnp.int32)
    total = lax.optimization_barrier(jnp.sum(fragment_local.astype(jnp.float32), axis=0))
    mean_local = total / N_REP
    glob = lax.dynamic_index_in_dim(global_params, index, 0, keepdims=False)
    moment = 0.9 * lax.dynamic_index_in_dim(outer_moment, index, 0, keepdims=False) + (glob - mean_local)
    updated = glob - 0.7 * (glob - mean_local + 0.9 * moment)
    picked = (jnp.arange(FRAGS, dtype=jnp.int32) == index)[:, None, None]
    new_global = jnp.where(picked, updated[None], global_params)
    new_outer = jnp.where(picked, moment[None], outer_moment)
    new_fragment = jnp.broadcast_to(updated.astype(jnp.bfloat16)[None], (N_REP, D, KV))
    return (new_weight, new_first, new_second, new_fragment, new_global, new_outer)
```

```python
import math

import jax
import jax.numpy as jnp
from jax import lax
from jax.experimental import pallas as pl
from jax.experimental.pallas import tpu as pltpu
from jax.sharding import PartitionSpec as P

CHUNKS = 2
NX = 4
NZ = 4
NY = 4
VMEM = 48 * 2**20

f32 = jnp.float32
bf16 = jnp.bfloat16


def along_x(value, step):
    pairs = [(a * NX + b, a * NX + (b + step) % NX) for a in range(NZ) for b in range(NX)]
    return lax.ppermute(value, "fsdp", pairs)


def along_z(value, step):
    pairs = [(a * NX + b, (a + step) % NZ * NX + b) for a in range(NZ) for b in range(NX)]
    return lax.ppermute(value, "fsdp", pairs)


def along_y(value, step):
    pairs = [(y * 4 + r, (y + step) % NY * 4 + r) for y in range(NY) for r in range(4)]
    return lax.ppermute(value, "rep", pairs)


def swap_core(value):
    return lax.ppermute(value, "rep", [(r, r ^ 1) for r in range(16)])


def swap_pair(value):
    return lax.ppermute(value, "rep", [(r, r ^ 2) for r in range(16)])


def pack_tokens(tokens):
    rows, width = tokens.shape
    block = width // (NX * NZ)
    me = lax.axis_index("fsdp")
    place = jnp.stack([me // NX, me % NX]).astype(jnp.int32)

    def copy(place_ref, *refs):
        for source, target in zip(refs[:NX], refs[NX:]):
            target[...] = source[...]

    def source(k):
        return pl.BlockSpec(
            (rows, block),
            lambda j, place: (0, (place[0] + j) % NZ * NX + (place[1] + k) % NX),
        )

    return pl.pallas_call(
        copy,
        grid_spec=pltpu.PrefetchScalarGridSpec(
            num_scalar_prefetch=1,
            grid=(NZ,),
            in_specs=[source(k) for k in range(NX)],
            out_specs=[pl.BlockSpec((rows, block), lambda j, place: (0, j))] * NX,
        ),
        out_shape=[jax.ShapeDtypeStruct((rows, NZ * block), tokens.dtype)] * NX,
        cost_estimate=pl.CostEstimate(
            flops=0, bytes_accessed=2 * tokens.size * 2, transcendentals=0
        ),
        name="pack_tokens",
    )(place, *[tokens] * NX)


def transpose_tokens(pieces):
    rows, width = pieces[0].shape

    def kernel(*refs):
        out = refs[-1]
        for k in range(NX):
            out[:, k * rows : (k + 1) * rows] = refs[k][...].T

    block = width // NZ
    return pl.pallas_call(
        kernel,
        grid=(NZ,),
        in_specs=[pl.BlockSpec((rows, block), lambda j: (0, j))] * NX,
        out_specs=pl.BlockSpec((block, NX * rows), lambda j: (j, 0)),
        out_shape=jax.ShapeDtypeStruct((width, NX * rows), bf16),
        compiler_params=pltpu.CompilerParams(vmem_limit_bytes=VMEM),
        cost_estimate=pl.CostEstimate(
            flops=0, bytes_accessed=4 * rows * width * NX, transcendentals=0
        ),
        name="transpose_tokens",
    )(*pieces)


def partial_keys(pieces, blocks):
    rows, width = pieces[0].shape
    columns = blocks[0].shape[1]

    def kernel(*refs):
        tokens = refs[:NX]
        weights = refs[NX : NX + len(blocks)]
        outs = refs[NX + len(blocks) : -1]
        whole = refs[-1]
        at = 0
        for ref in weights:
            whole[at : at + ref.shape[0], :] = ref[...]
            at += ref.shape[0]
        for k in (1, 2, 3, 0):
            outs[k][...] = jnp.dot(
                tokens[k][...], whole[...], preferred_element_type=f32
            ).astype(outs[k].dtype)

    return pl.pallas_call(
        kernel,
        out_shape=[
            jax.ShapeDtypeStruct((rows, columns), f32 if k == 0 else bf16) for k in range(NX)
        ],
        scratch_shapes=[pltpu.VMEM((width, columns), bf16)],
        compiler_params=pltpu.CompilerParams(vmem_limit_bytes=VMEM),
        cost_estimate=pl.CostEstimate(
            flops=2 * NX * rows * width * columns,
            bytes_accessed=2 * NX * rows * width + 2 * width * columns + 10 * rows * columns,
            transcendentals=0,
        ),
        name="partial_keys",
    )(*pieces, *blocks)


def partial_grad(turned, resids):
    width, tokens = turned.shape
    rows, columns = resids[0].shape
    block = width // NZ
    half = block // 2

    def kernel(turned_ref, *refs):
        resid = refs[:NX]
        own, one, far_a, far_b, three, whole = refs[NX:]
        for k in range(NX):
            whole[k * rows : (k + 1) * rows, :] = resid[k][...]
        far = jnp.dot(
            turned_ref[2 * block : 3 * block, :], whole[...], preferred_element_type=f32
        )
        far_a[...] = far[:half].astype(bf16)
        far_b[...] = far[half:].astype(bf16)
        for j, out in ((1, one), (3, three), (0, own)):
            out[...] = jnp.dot(
                turned_ref[j * block : (j + 1) * block, :], whole[...], preferred_element_type=f32
            ).astype(out.dtype)

    return pl.pallas_call(
        kernel,
        out_shape=[
            jax.ShapeDtypeStruct((block, columns), f32),
            jax.ShapeDtypeStruct((block, columns), bf16),
            jax.ShapeDtypeStruct((half, columns), bf16),
            jax.ShapeDtypeStruct((half, columns), bf16),
            jax.ShapeDtypeStruct((block, columns), bf16),
        ],
        scratch_shapes=[pltpu.VMEM((tokens, columns), bf16)],
        compiler_params=pltpu.CompilerParams(vmem_limit_bytes=VMEM),
        cost_estimate=pl.CostEstimate(
            flops=2 * tokens * width * columns,
            bytes_accessed=2 * tokens * width + 2 * tokens * columns + 10 * block * columns,
            transcendentals=0,
        ),
        name="partial_grad",
    )(turned, *resids)


def adam_columns(part, parts, scale, own, left, right, weight, first, second, earlier):
    rows, width = weight.shape
    columns = width // parts
    tile = rows // 3

    def kernel(own, left, right, weight, first, second, *refs):
        new_weight, new_first, new_second = refs[-3:]
        grad = (own[...] + left[...].astype(f32) + right[...].astype(f32)) * scale
        moved = 0.9 * first[...] + 0.1 * grad
        spread = 0.95 * second[...] + 0.05 * grad * grad
        wide = weight[...].astype(f32)
        new_first[...] = moved
        new_second[...] = spread
        new_weight[...] = (wide - 0.3 * (moved / (jnp.sqrt(spread) + 1e-08) + 0.1 * wide)).astype(
            bf16
        )

    piece = pl.BlockSpec((tile, columns), lambda i: (i, 0))
    place = pl.BlockSpec((tile, columns), lambda i: (i, part))
    aliases = {6 + n: n for n in range(3)} if earlier else {}
    return pl.pallas_call(
        kernel,
        grid=(3,),
        in_specs=[piece] * 3
        + [place] * 3
        + [pl.BlockSpec(memory_space=pl.ANY)] * (3 if earlier else 0),
        out_specs=[place] * 3,
        out_shape=[
            jax.ShapeDtypeStruct((rows, width), bf16),
            jax.ShapeDtypeStruct((rows, width), f32),
            jax.ShapeDtypeStruct((rows, width), f32),
        ],
        input_output_aliases=aliases,
        compiler_params=pltpu.CompilerParams(vmem_limit_bytes=VMEM),
        cost_estimate=pl.CostEstimate(
            flops=16 * rows * columns,
            bytes_accessed=28 * rows * columns,
            transcendentals=2 * rows * columns,
        ),
        name="adam_columns",
    )(own, left, right, weight, first, second, *(earlier or ()))


def gather_weight(shard):
    half = shard.shape[0] // 2
    previous = along_z(shard, 1)
    following = along_z(shard, -1)
    far_a = along_z(previous[:half], 1)
    far_b = along_z(following[half:], -1)
    return [shard, following, far_a, far_b, previous]


def inner_update(tokens, targets, weight, moment_first, moment_second):
    shard = weight[0]
    width = tokens.shape[1]
    inv_root = 1.0 / math.sqrt(width)
    scale = 1.0 / math.sqrt(tokens.shape[0] * lax.axis_size("fsdp"))
    columns = shard.shape[1] // CHUNKS

    blocks = [
        gather_weight(shard[:, c * columns : (c + 1) * columns]) for c in range(CHUNKS)
    ]
    pieces = pack_tokens(tokens)
    pieces = [pieces[0]] + [along_x(pieces[k], k) for k in range(1, NX)]
    keys = [partial_keys(pieces, blocks[c]) for c in range(CHUNKS)]
    turned = transpose_tokens(pieces)
    outs = None
    for c in range(CHUNKS):
        own = keys[c][0]
        others = [along_x(keys[c][k], -k) for k in range(1, NX)]
        total = own
        for other in others:
            total = total + other.astype(f32)
        goals = targets[:, c * columns : (c + 1) * columns].astype(f32)
        resid = (total * inv_root - goals).astype(bf16)
        resids = [resid] + [along_x(resid, k) for k in range(1, NX)]
        mine, one, far_a, far_b, three = partial_grad(turned, resids)
        half = far_a.shape[0]
        far_a = along_z(far_a, 1)
        far_b = along_z(far_b, -1)
        one = jnp.concatenate(
            [(one[:half].astype(f32) + far_a.astype(f32)).astype(bf16), one[half:]]
        )
        three = jnp.concatenate(
            [three[:half], (three[half:].astype(f32) + far_b.astype(f32)).astype(bf16)]
        )
        left = along_z(one, 1)
        right = along_z(three, -1)
        outs = adam_columns(
            c,
            CHUNKS,
            scale,
            mine,
            left,
            right,
            shard,
            moment_first[0],
            moment_second[0],
            outs,
        )
    new_weight, new_first, new_second = outs
    return (new_weight[None], new_first[None], new_second[None])


def outer_update(fragment_local, global_params, outer_moment, fragment):
    rows = fragment_local.shape[1]
    me = lax.axis_index("rep")
    y, pair, core = me // 4, me // 2 % 2, me % 2
    pick = lax.dynamic_index_in_dim
    local = fragment_local[0].T.reshape(NY, 2, 2, -1, rows)
    total = pick(local, core, 2, keepdims=False).astype(f32) + swap_core(
        pick(local, 1 - core, 2, keepdims=False)
    ).astype(f32)
    kept = pick(total, y, 0, keepdims=False)
    for step in range(1, NY):
        kept = kept + along_y(pick(total, (y + step) % NY, 0, keepdims=False), step)
    total = pick(kept, pair, 0, keepdims=False) + swap_pair(
        pick(kept, 1 - pair, 0, keepdims=False)
    )
    mean_local = total / lax.axis_size("rep")
    index = fragment[0]
    globs = jnp.swapaxes(global_params, 1, 2)
    outers = jnp.swapaxes(outer_moment, 1, 2)
    glob = pick(globs, index, 0, keepdims=False)
    moment = 0.9 * pick(outers, index, 0, keepdims=False) + (glob - mean_local)
    updated = glob - 0.7 * (glob - mean_local + 0.9 * moment)
    picked = (lax.iota(jnp.int32, global_params.shape[0]) == index)[:, None, None]
    new_global = jnp.swapaxes(jnp.where(picked, updated[None], globs), 1, 2)
    new_outer = jnp.swapaxes(jnp.where(picked, moment[None], outers), 1, 2)

    mine = updated.astype(bf16)
    other = swap_pair(mine)
    both = jnp.where(pair == 0, jnp.stack([mine, other]), jnp.stack([other, mine]))
    parts = [both] + [along_y(both, step) for step in range(1, NY)]
    stacked = jnp.stack(parts[:1] + parts[:0:-1])
    ordered = jnp.concatenate([stacked, stacked])
    half = lax.dynamic_slice_in_dim(ordered, (NY - y) % NY, NY, 0)
    other = swap_core(half)
    whole = jnp.where(
        core == 0, jnp.stack([half, other], 2), jnp.stack([other, half], 2)
    )
    whole = whole.reshape(-1, rows).T
    return (whole[None], new_global, new_outer)


def body(
    tokens,
    targets,
    weight,
    moment_first,
    moment_second,
    fragment_local,
    global_params,
    outer_moment,
    fragment,
):
    new_weight, new_first, new_second = inner_update(
        tokens, targets, weight, moment_first, moment_second
    )
    new_fragment, new_global, new_outer = outer_update(
        fragment_local, global_params, outer_moment, fragment
    )
    return (new_weight, new_first, new_second, new_fragment, new_global, new_outer)


def solution(mesh):
    return jax.shard_map(
        body,
        mesh=mesh,
        in_specs=(
            P(("rep", "fsdp"), None),
            P(("rep", "fsdp"), None),
            P("rep", "fsdp", None),
            P("rep", "fsdp", None),
            P("rep", "fsdp", None),
            P("rep", "fsdp", None),
            P(None, "fsdp", "rep"),
            P(None, "fsdp", "rep"),
            P(),
        ),
        out_specs=(
            P("rep", "fsdp", None),
            P("rep", "fsdp", None),
            P("rep", "fsdp", None),
            P("rep", "fsdp", None),
            P(None, "fsdp", "rep"),
            P(None, "fsdp", "rep"),
        ),
        check_vma=False,
    )
```

```python
import math

import jax
import jax.numpy as jnp
from jax import lax
from jax.experimental import pallas as pl
from jax.experimental.pallas import tpu as pltpu
from jax.sharding import PartitionSpec as P

CHUNKS = 2
NX = 4
NZ = 4
NY = 4
LIMIT = 16 * 2**20
LIGHT = pl.CostEstimate(flops=1, bytes_accessed=1, transcendentals=0)
HEAVY = pl.CostEstimate(flops=4 * 10**10, bytes_accessed=10**6, transcendentals=0)

f32 = jnp.float32
bf16 = jnp.bfloat16


def along_x(value, step):
    pairs = [(a * NX + b, a * NX + (b + step) % NX) for a in range(NZ) for b in range(NX)]
    return lax.ppermute(value, "fsdp", pairs)


def along_z(value, step):
    pairs = [(a * NX + b, (a + step) % NZ * NX + b) for a in range(NZ) for b in range(NX)]
    return lax.ppermute(value, "fsdp", pairs)


def along_y(value, step):
    pairs = [(y * 4 + r, (y + step) % NY * 4 + r) for y in range(NY) for r in range(4)]
    return lax.ppermute(value, "rep", pairs)


def swap_core(value):
    return lax.ppermute(value, "rep", [(r, r ^ 1) for r in range(16)])


def swap_pair(value):
    return lax.ppermute(value, "rep", [(r, r ^ 2) for r in range(16)])


def kernel_call(kernel, inputs, outs, cost, name, scratch=(), blocked=None, **options):
    blocked = blocked or {}
    specs = [
        blocked.get(n, pl.BlockSpec(memory_space=pltpu.VMEM)) for n in range(len(inputs))
    ]
    inputs = [
        value if n in blocked else pltpu.with_memory_space_constraint(value, pltpu.VMEM)
        for n, value in enumerate(inputs)
    ]
    return pl.pallas_call(
        kernel,
        in_specs=specs,
        out_specs=[pl.BlockSpec(memory_space=pltpu.VMEM)] * len(outs),
        out_shape=[pltpu.VMEM(shape, dtype) for shape, dtype in outs],
        scratch_shapes=list(scratch),
        compiler_params=pltpu.CompilerParams(vmem_limit_bytes=LIMIT),
        cost_estimate=cost,
        name=name,
        **options,
    )(*inputs)


SMALL = pl.BlockSpec(memory_space=pltpu.SMEM)
ANYWHERE = pl.BlockSpec(memory_space=pl.ANY)


def pack_tokens(tokens):
    rows, width = tokens.shape
    block = width // (NX * NZ)
    me = lax.axis_index("fsdp").astype(jnp.int32).reshape(1)

    def kernel(me_ref, source, *refs):
        sems = refs[-1]
        z, x = me_ref[0] // NX, me_ref[0] % NX
        copies = []
        for k in range(NX):
            for j in range(NZ):
                start = ((z + j) % NZ * NX + (x + k) % NX) * block
                copies.append(
                    pltpu.make_async_copy(
                        source.at[:, pl.ds(pl.multiple_of(start, 128), block)],
                        refs[k].at[:, j * block : (j + 1) * block],
                        sems.at[k, j],
                    )
                )
        for copy in copies:
            copy.start()
        for copy in copies:
            copy.wait()

    return kernel_call(
        kernel,
        [me, tokens],
        [((rows, NZ * block), tokens.dtype)] * NX,
        LIGHT,
        "pack_tokens",
        scratch=[pltpu.SemaphoreType.DMA((NX, NZ))],
        blocked={0: SMALL, 1: ANYWHERE},
    )


def load(arrays, name):
    count = len(arrays)

    def kernel(*refs):
        copies = [
            pltpu.make_async_copy(refs[n], refs[count + n], refs[-1].at[n]) for n in range(count)
        ]
        for copy in copies:
            copy.start()
        for copy in copies:
            copy.wait()

    return kernel_call(
        kernel,
        arrays,
        [(array.shape, array.dtype) for array in arrays],
        LIGHT,
        name,
        scratch=[pltpu.SemaphoreType.DMA((count,))],
        blocked={n: ANYWHERE for n in range(count)},
    )


def transpose_tokens(pieces):
    rows, width = pieces[0].shape

    def kernel(*refs):
        out = refs[-1]
        for k in range(NX):
            out[:, k * rows : (k + 1) * rows] = refs[k][...].T

    return kernel_call(
        kernel, pieces, [((width, NX * rows), bf16)], HEAVY, "transpose_tokens"
    )[0]


def transpose(value, name, cost):
    def kernel(source, out):
        out[...] = source[...].T

    return kernel_call(kernel, [value], [(value.shape[::-1], value.dtype)], cost, name)[0]


def split_columns(value, parts):
    rows, width = value.shape
    columns = width // parts

    def kernel(source, *refs):
        copies = [
            pltpu.make_async_copy(
                source.at[:, c * columns : (c + 1) * columns], refs[c], refs[-1].at[c]
            )
            for c in range(parts)
        ]
        for copy in copies:
            copy.start()
        for copy in copies:
            copy.wait()

    return kernel_call(
        kernel,
        [value],
        [((rows, columns), value.dtype)] * parts,
        LIGHT,
        "split_columns",
        scratch=[pltpu.SemaphoreType.DMA((parts,))],
        blocked={0: ANYWHERE},
    )


def outer_halves(previous, following):
    half = previous.shape[0] // 2

    def kernel(previous, following, top, bottom):
        top[...] = previous[:half, :]
        bottom[...] = following[half:, :]

    return kernel_call(
        kernel, [previous, following], [((half, previous.shape[1]), bf16)] * 2, LIGHT, "outer_halves"
    )


def partial_keys(pieces, blocks):
    rows, width = pieces[0].shape
    columns = blocks[0].shape[1]

    def kernel(*refs):
        tokens = refs[:NX]
        weights = refs[NX : NX + len(blocks)]
        outs = refs[NX + len(blocks) : -1]
        whole = refs[-1]
        at = 0
        for ref in weights:
            whole[at : at + ref.shape[0], :] = ref[...]
            at += ref.shape[0]
        for k in (2, 1, 3, 0):
            outs[k][...] = jnp.dot(
                tokens[k][...], whole[...], preferred_element_type=f32
            ).astype(outs[k].dtype)

    return kernel_call(
        kernel,
        [*pieces, *blocks],
        [((rows, columns), f32 if k == 0 else bf16) for k in range(NX)],
        HEAVY,
        "partial_keys",
        scratch=[pltpu.VMEM((width, columns), bf16)],
    )


def residual(own, others, goals, part, inv_root):
    chosen = slice(part * own.shape[1], (part + 1) * own.shape[1])

    def kernel(own, one, two, three, goals, out):
        total = own[...] + one[...].astype(f32) + two[...].astype(f32) + three[...].astype(f32)
        out[...] = (total * inv_root - goals[:, chosen].astype(f32)).astype(bf16)

    return kernel_call(kernel, [own, *others, goals], [(own.shape, bf16)], LIGHT, "residual")[0]


def partial_grad(turned, resids):
    width, tokens = turned.shape
    rows, columns = resids[0].shape
    block = width // NZ
    half = block // 2

    def kernel(turned_ref, *refs):
        resid = refs[:NX]
        own, one, far_a, far_b, three, whole = refs[NX:]
        for k in range(NX):
            whole[k * rows : (k + 1) * rows, :] = resid[k][...]
        far = jnp.dot(
            turned_ref[2 * block : 3 * block, :], whole[...], preferred_element_type=f32
        )
        far_a[...] = far[:half].astype(bf16)
        far_b[...] = far[half:].astype(bf16)
        for j, out in ((1, one), (3, three), (0, own)):
            out[...] = jnp.dot(
                turned_ref[j * block : (j + 1) * block, :], whole[...], preferred_element_type=f32
            ).astype(out.dtype)

    return kernel_call(
        kernel,
        [turned, *resids],
        [
            ((block, columns), f32),
            ((block, columns), bf16),
            ((half, columns), bf16),
            ((half, columns), bf16),
            ((block, columns), bf16),
        ],
        HEAVY,
        "partial_grad",
        scratch=[pltpu.VMEM((tokens, columns), bf16)],
    )


def add_halves(one, far_a, three, far_b):
    half = far_a.shape[0]

    def kernel(one, far_a, three, far_b, up, down):
        up[:half, :] = (one[:half, :].astype(f32) + far_a[...].astype(f32)).astype(bf16)
        up[half:, :] = one[half:, :]
        down[:half, :] = three[:half, :]
        down[half:, :] = (three[half:, :].astype(f32) + far_b[...].astype(f32)).astype(bf16)

    return kernel_call(
        kernel, [one, far_a, three, far_b], [(one.shape, bf16)] * 2, LIGHT, "add_halves"
    )


def adam_columns(part, parts, scale, own, left, right, weight, first, second, earlier):
    rows, width = weight.shape
    columns = width // parts
    tiles = 3
    tile = rows // tiles
    chosen = slice(part * columns, (part + 1) * columns)

    def kernel(own, left, right, weight, first, second, *refs):
        new_weight, new_first, new_second = refs[-3:]
        at = pl.ds(pl.multiple_of(pl.program_id(0) * tile, tile), tile)
        grad = (own[at, :] + left[at, :].astype(f32) + right[at, :].astype(f32)) * scale
        moved = 0.9 * first[at, chosen] + 0.1 * grad
        spread = 0.95 * second[at, chosen] + 0.05 * grad * grad
        wide = weight[at, chosen].astype(f32)
        new_first[...] = moved
        new_second[...] = spread
        new_weight[...] = (wide - 0.3 * (moved / (jnp.sqrt(spread) + 1e-08) + 0.1 * wide)).astype(
            bf16
        )

    inputs = [own, left, right, weight, first, second]
    place = pl.BlockSpec((tile, columns), lambda i: (i, part))
    return pl.pallas_call(
        kernel,
        grid=(tiles,),
        in_specs=[pl.BlockSpec(memory_space=pltpu.VMEM)] * 6
        + [ANYWHERE] * (3 if earlier else 0),
        out_specs=[place] * 3,
        out_shape=[
            jax.ShapeDtypeStruct((rows, width), bf16),
            jax.ShapeDtypeStruct((rows, width), f32),
            jax.ShapeDtypeStruct((rows, width), f32),
        ],
        input_output_aliases={6 + n: n for n in range(3)} if earlier else {},
        compiler_params=pltpu.CompilerParams(vmem_limit_bytes=LIMIT),
        cost_estimate=LIGHT,
        name="adam_columns",
    )(*[pltpu.with_memory_space_constraint(value, pltpu.VMEM) for value in inputs], *(earlier or ()))


class Outer:
    def __init__(self, fragment_local, global_params, outer_moment, fragment):
        self.given = (fragment_local, global_params, outer_moment, fragment)
        me = lax.axis_index("rep")
        self.y, self.pair, self.core = me // 4, me // 2 % 2, me % 2

    def swap_cores(self, *since):
        rows = self.given[0].shape[1]
        turned = transpose(tie([self.given[0][0]], *since)[0], "turn_fragment", LIGHT)
        local = turned.reshape(NY, 2, 2, -1, rows)
        self.state = pick(local, self.core, 2).astype(f32) + swap_core(
            pick(local, 1 - self.core, 2)
        ).astype(f32)

    def reduce_y(self):
        total = self.state
        kept = pick(total, self.y, 0)
        for step in range(1, NY):
            kept = kept + along_y(pick(total, (self.y + step) % NY, 0), step)
        self.state = kept

    def reduce_pair(self, *since):
        _, global_params, outer_moment, fragment = self.given
        kept = tie([self.state], *since)[0]
        total = pick(kept, self.pair, 0) + swap_pair(pick(kept, 1 - self.pair, 0))
        mean_local = total / lax.axis_size("rep")
        index = fragment[0]
        globs = jnp.swapaxes(global_params, 1, 2)
        outers = jnp.swapaxes(outer_moment, 1, 2)
        glob = pick(globs, index, 0)
        moment = 0.9 * pick(outers, index, 0) + (glob - mean_local)
        updated = glob - 0.7 * (glob - mean_local + 0.9 * moment)
        picked = (lax.iota(jnp.int32, global_params.shape[0]) == index)[:, None, None]
        self.new_global = jnp.swapaxes(jnp.where(picked, updated[None], globs), 1, 2)
        self.new_outer = jnp.swapaxes(jnp.where(picked, moment[None], outers), 1, 2)
        self.state = updated.astype(bf16)

    def gather_pair(self, *since):
        mine = tie([self.state], *since)[0]
        other = swap_pair(mine)
        self.state = jnp.where(
            self.pair == 0, jnp.stack([mine, other]), jnp.stack([other, mine])
        )

    def gather_y(self):
        both = self.state
        parts = [both] + [along_y(both, step) for step in range(1, NY)]
        stacked = jnp.stack(parts[:1] + parts[:0:-1])
        ordered = jnp.concatenate([stacked, stacked])
        self.state = lax.dynamic_slice_in_dim(ordered, (NY - self.y) % NY, NY, 0)

    def gather_cores(self):
        mine = self.state
        other = swap_core(mine)
        whole = jnp.where(
            self.core == 0, jnp.stack([mine, other], 2), jnp.stack([other, mine], 2)
        )
        self.state = whole.reshape(-1, whole.shape[-1]).T

    def results(self):
        return (self.state[None], self.new_global, self.new_outer)


def pick(value, index, axis):
    return lax.dynamic_index_in_dim(value, index, axis, keepdims=False)


def tie(values, *others):
    return lax.optimization_barrier((tuple(values), others))[0]


def body(
    tokens,
    targets,
    weight,
    moment_first,
    moment_second,
    fragment_local,
    global_params,
    outer_moment,
    fragment,
):
    outer = Outer(fragment_local, global_params, outer_moment, fragment)
    shard = weight[0]
    width = tokens.shape[1]
    inv_root = 1.0 / math.sqrt(width)
    scale = 1.0 / math.sqrt(tokens.shape[0] * lax.axis_size("fsdp"))

    owns = split_columns(shard, CHUNKS)
    blocks = [[own, along_z(own, -1), along_z(own, 1)] for own in owns]
    pieces = pack_tokens(tokens)
    far = {k: along_x(pieces[k], k) for k in (2, 1, 3)}
    pieces = [pieces[0], far[1], far[2], far[3]]
    for block in blocks:
        top, bottom = outer_halves(block[2], block[1])
        block[2:] = [along_z(top, 1), along_z(bottom, -1), block[2]]

    def back(keys):
        return {k: along_x(keys[k], -k) for k in (2, 1, 3)}

    def out(keys, got, part):
        resid = residual(keys[0], [got[1], got[2], got[3]], targets, part, inv_root)
        there = {k: along_x(resid, k) for k in (2, 1, 3)}
        return [resid, there[1], there[2], there[3]]

    keys = partial_keys(pieces, blocks[0])
    got = back(keys)
    outer.swap_cores(keys[0])
    outer.reduce_y()
    turned = transpose_tokens(tie(pieces, keys[0]))
    resids = out(keys, got, 0)

    keys = partial_keys(pieces, tie(blocks[1], resids[0]))
    got = back(keys)
    outer.reduce_pair(keys[0])
    outer.gather_pair()

    own, one, far_a, far_b, three = partial_grad(turned, resids)
    far_a, far_b = along_z(far_a, 1), along_z(far_b, -1)
    resids = out(keys, got, 1)
    staged = load(tie([shard, moment_first[0], moment_second[0]], resids[0]), "load_state")
    outer.gather_y()

    up, down = add_halves(one, far_a, three, far_b)
    left, right = along_z(up, 1), along_z(down, -1)

    own1, one1, far_a, far_b, three1 = partial_grad(turned, tie(resids, up))
    far_a, far_b = along_z(far_a, 1), along_z(far_b, -1)
    up, down = add_halves(one1, far_a, three1, far_b)
    left1, right1 = along_z(up, 1), along_z(down, -1)
    outer.gather_cores()
    outs = adam_columns(0, CHUNKS, scale, own, left, right, *staged, None)
    outs = adam_columns(1, CHUNKS, scale, own1, left1, right1, *staged, outs)
    new_weight, new_first, new_second = outs
    return (new_weight[None], new_first[None], new_second[None], *outer.results())


def solution(mesh):
    return jax.shard_map(
        body,
        mesh=mesh,
        in_specs=(
            P(("rep", "fsdp"), None),
            P(("rep", "fsdp"), None),
            P("rep", "fsdp", None),
            P("rep", "fsdp", None),
            P("rep", "fsdp", None),
            P("rep", "fsdp", None),
            P(None, "fsdp", "rep"),
            P(None, "fsdp", "rep"),
            P(),
        ),
        out_specs=(
            P("rep", "fsdp", None),
            P("rep", "fsdp", None),
            P("rep", "fsdp", None),
            P("rep", "fsdp", None),
            P(None, "fsdp", "rep"),
            P(None, "fsdp", "rep"),
        ),
        check_vma=False,
    )
```

```python
import math

import jax
import jax.numpy as jnp
from jax import lax
from jax.experimental import pallas as pl
from jax.experimental.pallas import tpu as pltpu
from jax.sharding import PartitionSpec as P

CHUNKS = 2
NX = 4
NZ = 4
NY = 4
LIMIT = 16 * 2**20
LIGHT = pl.CostEstimate(flops=1, bytes_accessed=1, transcendentals=0)
HEAVY = pl.CostEstimate(flops=4 * 10**10, bytes_accessed=10**6, transcendentals=0)

f32 = jnp.float32
bf16 = jnp.bfloat16


def along_x(value, step):
    pairs = [(a * NX + b, a * NX + (b + step) % NX) for a in range(NZ) for b in range(NX)]
    return lax.ppermute(value, "fsdp", pairs)


def along_z(value, step):
    pairs = [(a * NX + b, (a + step) % NZ * NX + b) for a in range(NZ) for b in range(NX)]
    return lax.ppermute(value, "fsdp", pairs)


def swap_near(value):
    return lax.ppermute(value, "rep", [(r, r ^ 4) for r in range(16)])


def swap_far(value):
    return lax.ppermute(value, "rep", [(r, r ^ 8) for r in range(16)])


def swap_core(value):
    return lax.ppermute(value, "rep", [(r, r ^ 1) for r in range(16)])


def swap_pair(value):
    return lax.ppermute(value, "rep", [(r, r ^ 2) for r in range(16)])


def kernel_call(kernel, inputs, outs, cost, name, scratch=(), blocked=None, **options):
    blocked = blocked or {}
    specs = [
        blocked.get(n, pl.BlockSpec(memory_space=pltpu.VMEM)) for n in range(len(inputs))
    ]
    inputs = [
        value if n in blocked else pltpu.with_memory_space_constraint(value, pltpu.VMEM)
        for n, value in enumerate(inputs)
    ]
    return pl.pallas_call(
        kernel,
        in_specs=specs,
        out_specs=[pl.BlockSpec(memory_space=pltpu.VMEM)] * len(outs),
        out_shape=[pltpu.VMEM(shape, dtype) for shape, dtype in outs],
        scratch_shapes=list(scratch),
        compiler_params=pltpu.CompilerParams(vmem_limit_bytes=LIMIT),
        cost_estimate=cost,
        name=name,
        **options,
    )(*inputs)


SMALL = pl.BlockSpec(memory_space=pltpu.SMEM)
ANYWHERE = pl.BlockSpec(memory_space=pl.ANY)
IN_HBM = pl.BlockSpec(memory_space=pltpu.HBM)


def in_hbm(value):
    return pltpu.with_memory_space_constraint(value, pltpu.HBM)


def pack_tokens(tokens):
    rows, width = tokens.shape
    block = width // (NX * NZ)
    me = lax.axis_index("fsdp").astype(jnp.int32).reshape(1)

    def kernel(me_ref, source, *refs):
        sems = refs[-1]
        z, x = me_ref[0] // NX, me_ref[0] % NX
        copies = []
        for k in range(NX):
            for j in range(NZ):
                start = ((z + j) % NZ * NX + (x + k) % NX) * block
                copies.append(
                    pltpu.make_async_copy(
                        source.at[:, pl.ds(pl.multiple_of(start, 128), block)],
                        refs[k].at[:, j * block : (j + 1) * block],
                        sems.at[k, j],
                    )
                )
        for copy in copies:
            copy.start()
        for copy in copies:
            copy.wait()

    return kernel_call(
        kernel,
        [me, tokens],
        [((rows, NZ * block), tokens.dtype)] * NX,
        LIGHT,
        "pack_tokens",
        scratch=[pltpu.SemaphoreType.DMA((NX, NZ))],
        blocked={0: SMALL, 1: ANYWHERE},
    )


def load(arrays, name):
    count = len(arrays)

    def kernel(*refs):
        copies = [
            pltpu.make_async_copy(refs[n], refs[count + n], refs[-1].at[n]) for n in range(count)
        ]
        for copy in copies:
            copy.start()
        for copy in copies:
            copy.wait()

    return kernel_call(
        kernel,
        [in_hbm(array) for array in arrays],
        [(array.shape, array.dtype) for array in arrays],
        LIGHT,
        name,
        scratch=[pltpu.SemaphoreType.DMA((count,))],
        blocked={n: IN_HBM for n in range(count)},
    )


def transpose_tokens(pieces):
    rows, width = pieces[0].shape

    def kernel(*refs):
        out = refs[-1]
        for k in range(NX):
            out[:, k * rows : (k + 1) * rows] = refs[k][...].T

    return kernel_call(
        kernel, pieces, [((width, NX * rows), bf16)], HEAVY, "transpose_tokens"
    )[0]


def split_columns(value, parts):
    rows, width = value.shape
    columns = width // parts

    def kernel(source, *refs):
        copies = [
            pltpu.make_async_copy(
                source.at[:, c * columns : (c + 1) * columns], refs[c], refs[-1].at[c]
            )
            for c in range(parts)
        ]
        for copy in copies:
            copy.start()
        for copy in copies:
            copy.wait()

    return kernel_call(
        kernel,
        [value],
        [((rows, columns), value.dtype)] * parts,
        LIGHT,
        "split_columns",
        scratch=[pltpu.SemaphoreType.DMA((parts,))],
        blocked={0: ANYWHERE},
    )


def outer_halves(previous, following):
    half = previous.shape[0] // 2

    def kernel(previous, following, top, bottom):
        top[...] = previous[:half, :]
        bottom[...] = following[half:, :]

    return kernel_call(
        kernel, [previous, following], [((half, previous.shape[1]), bf16)] * 2, LIGHT, "outer_halves"
    )


def partial_keys(pieces, blocks, cost):
    rows, width = pieces[0].shape
    columns = blocks[0].shape[1]

    def kernel(*refs):
        tokens = refs[:NX]
        weights = refs[NX : NX + len(blocks)]
        outs = refs[NX + len(blocks) : -1]
        whole = refs[-1]
        at = 0
        for ref in weights:
            whole[at : at + ref.shape[0], :] = ref[...]
            at += ref.shape[0]
        for k in (2, 1, 3, 0):
            outs[k][...] = jnp.dot(
                tokens[k][...], whole[...], preferred_element_type=f32
            ).astype(outs[k].dtype)

    return kernel_call(
        kernel,
        [*pieces, *blocks],
        [((rows, columns), f32 if k == 0 else bf16) for k in range(NX)],
        cost,
        "partial_keys",
        scratch=[pltpu.VMEM((width, columns), bf16)],
    )


def residual(own, others, goals, part, inv_root):
    chosen = slice(part * own.shape[1], (part + 1) * own.shape[1])

    def kernel(own, one, two, three, goals, out):
        total = own[...] + one[...].astype(f32) + two[...].astype(f32) + three[...].astype(f32)
        out[...] = (total * inv_root - goals[:, chosen].astype(f32)).astype(bf16)

    return kernel_call(kernel, [own, *others, goals], [(own.shape, bf16)], LIGHT, "residual")[0]


def partial_grad(turned, resids):
    width, tokens = turned.shape
    rows, columns = resids[0].shape
    block = width // NZ
    half = block // 2

    def kernel(turned_ref, *refs):
        resid = refs[:NX]
        own, one, far_a, far_b, three, whole = refs[NX:]
        for k in range(NX):
            whole[k * rows : (k + 1) * rows, :] = resid[k][...]
        far = jnp.dot(
            turned_ref[2 * block : 3 * block, :], whole[...], preferred_element_type=f32
        )
        far_a[...] = far[:half].astype(bf16)
        far_b[...] = far[half:].astype(bf16)
        for j, out in ((1, one), (3, three), (0, own)):
            out[...] = jnp.dot(
                turned_ref[j * block : (j + 1) * block, :], whole[...], preferred_element_type=f32
            ).astype(out.dtype)

    return kernel_call(
        kernel,
        [turned, *resids],
        [
            ((block, columns), f32),
            ((block, columns), bf16),
            ((half, columns), bf16),
            ((half, columns), bf16),
            ((block, columns), bf16),
        ],
        HEAVY,
        "partial_grad",
        scratch=[pltpu.VMEM((tokens, columns), bf16)],
    )


def add_halves(one, far_a, three, far_b):
    half = far_a.shape[0]

    def kernel(one, far_a, three, far_b, up, down):
        up[:half, :] = (one[:half, :].astype(f32) + far_a[...].astype(f32)).astype(bf16)
        up[half:, :] = one[half:, :]
        down[:half, :] = three[:half, :]
        down[half:, :] = (three[half:, :].astype(f32) + far_b[...].astype(f32)).astype(bf16)

    return kernel_call(
        kernel, [one, far_a, three, far_b], [(one.shape, bf16)] * 2, LIGHT, "add_halves"
    )


def adam_columns(part, parts, scale, own, left, right, weight, first, second, earlier):
    rows, width = weight.shape
    columns = width // parts
    tiles = 3
    tile = rows // tiles
    chosen = slice(part * columns, (part + 1) * columns)

    def kernel(own, left, right, weight, first, second, *refs):
        new_weight, new_first, new_second = refs[-3:]
        at = pl.ds(pl.multiple_of(pl.program_id(0) * tile, tile), tile)
        grad = (own[at, :] + left[at, :].astype(f32) + right[at, :].astype(f32)) * scale
        moved = 0.9 * first[at, chosen] + 0.1 * grad
        spread = 0.95 * second[at, chosen] + 0.05 * grad * grad
        wide = weight[at, chosen].astype(f32)
        new_first[...] = moved
        new_second[...] = spread
        new_weight[...] = (wide - 0.3 * (moved / (jnp.sqrt(spread) + 1e-08) + 0.1 * wide)).astype(
            bf16
        )

    inputs = [own, left, right, weight, first, second]
    place = pl.BlockSpec((tile, columns), lambda i: (i, part))
    return pl.pallas_call(
        kernel,
        grid=(tiles,),
        in_specs=[pl.BlockSpec(memory_space=pltpu.VMEM)] * 6
        + [ANYWHERE] * (3 if earlier else 0),
        out_specs=[place] * 3,
        out_shape=[
            jax.ShapeDtypeStruct((rows, width), bf16),
            jax.ShapeDtypeStruct((rows, width), f32),
            jax.ShapeDtypeStruct((rows, width), f32),
        ],
        input_output_aliases={6 + n: n for n in range(3)} if earlier else {},
        compiler_params=pltpu.CompilerParams(vmem_limit_bytes=LIMIT),
        cost_estimate=LIGHT,
        name="adam_columns",
    )(*[pltpu.with_memory_space_constraint(value, pltpu.VMEM) for value in inputs], *(earlier or ()))


def turn_fragment(fragment, core):
    rows, width = fragment.shape
    columns = width // 16

    def kernel(core_ref, source, mine, other):
        low = core_ref[0] == 0
        for y in range(NY):
            for pair in range(2):
                at = (y * 2 + pair) * 2 * columns
                both = source[:, at : at + 2 * columns].T
                mine[y, pair] = jnp.where(low, both[:columns], both[columns:])
                other[y, pair] = jnp.where(low, both[columns:], both[:columns])

    return kernel_call(
        kernel,
        [core, fragment],
        [((NY, 2, columns, rows), bf16)] * 2,
        LIGHT,
        "turn_fragment",
        blocked={0: SMALL},
    )


def halve(mine, other, keep, name):
    shape = (mine.shape[0] // 2, *mine.shape[1:])

    def kernel(keep_ref, mine, other, kept, sent):
        for out, which in ((sent, 1 - keep_ref[0]), (kept, keep_ref[0])):
            at = pl.ds(which * shape[0], shape[0])
            out[...] = mine[at].astype(f32) + other[at].astype(f32)

    return kernel_call(
        kernel,
        [keep, mine, other],
        [(shape, f32)] * 2,
        LIGHT,
        name,
        blocked={0: SMALL},
    )


def total(mine, other):
    def kernel(mine, other, out):
        out[...] = mine[...] + other[...]

    return kernel_call(kernel, [mine, other], [(mine.shape, f32)], LIGHT, "total")[0]


def stack(mine, other, second, name):
    count = mine.shape[0]

    def kernel(second_ref, mine, other, out):
        out[pl.ds(second_ref[0] * count, count)] = mine[...]
        out[pl.ds((1 - second_ref[0]) * count, count)] = other[...]

    return kernel_call(
        kernel,
        [second, mine, other],
        [((2 * count, *mine.shape[1:]), mine.dtype)],
        LIGHT,
        name,
        blocked={0: SMALL},
    )[0]


def chosen_params(globs, outers, index):
    def kernel(index_ref, globs, outers, out):
        out[0] = globs[index_ref[0]]
        out[1] = outers[index_ref[0]]

    return kernel_call(
        kernel,
        [index, globs, outers],
        [((2, *globs.shape[1:]), f32)],
        LIGHT,
        "chosen_params",
        blocked={0: SMALL},
    )[0]


def nesterov(mine, other, own, theirs, globs, outers, index, pair, replicas):
    frags = globs.shape[0]

    def kernel(index_ref, pair_ref, mine, other, own, theirs, globs, outers, *outs):
        updated, new_global, new_outer = outs
        new_global[...] = globs[...]
        new_outer[...] = outers[...]
        for which, params in ((pair_ref[0], own), (1 - pair_ref[0], theirs)):
            mean_local = (mine[which] + other[which]) / replicas
            glob = params[0]
            moment = 0.9 * params[1] + (glob - mean_local)
            after = glob - 0.7 * (glob - mean_local + 0.9 * moment)
            updated[which] = after.astype(bf16)
            if params is own:
                new_global[index_ref[0]] = after
                new_outer[index_ref[0]] = moment

    return pl.pallas_call(
        kernel,
        in_specs=[SMALL] * 2 + [pl.BlockSpec(memory_space=pltpu.VMEM)] * 6,
        out_specs=[pl.BlockSpec(memory_space=pltpu.VMEM)] + [pl.BlockSpec()] * 2,
        out_shape=[
            pltpu.VMEM(mine.shape, bf16),
            jax.ShapeDtypeStruct(globs.shape, f32),
            jax.ShapeDtypeStruct(globs.shape, f32),
        ],
        compiler_params=pltpu.CompilerParams(vmem_limit_bytes=LIMIT),
        cost_estimate=LIGHT,
        name="nesterov",
    )(
        index,
        pair,
        *[
            pltpu.with_memory_space_constraint(value, pltpu.VMEM)
            for value in (mine, other, own, theirs, globs, outers)
        ],
    )


def weave(mine, other, core):
    ys, pairs, columns, rows = mine.shape

    def kernel(core_ref, mine, other, out):
        low = core_ref[0] == 0
        for y in range(ys):
            for pair in range(pairs):
                a, b = mine[y, pair], other[y, pair]
                both = jnp.concatenate([jnp.where(low, a, b), jnp.where(low, b, a)])
                at = (y * pairs + pair) * 2 * columns
                out[:, at : at + 2 * columns] = both.T

    return pl.pallas_call(
        kernel,
        in_specs=[SMALL] + [pl.BlockSpec(memory_space=pltpu.VMEM)] * 2,
        out_shape=jax.ShapeDtypeStruct((rows, 2 * columns * ys * pairs), bf16),
        compiler_params=pltpu.CompilerParams(vmem_limit_bytes=LIMIT),
        cost_estimate=LIGHT,
        name="weave",
    )(core, *[pltpu.with_memory_space_constraint(v, pltpu.VMEM) for v in (mine, other)])


class Outer:
    def __init__(self, fragment_local, global_params, outer_moment, fragment):
        me = lax.axis_index("rep").astype(jnp.int32).reshape(1)
        self.far, self.near, self.pair, self.core = me // 8, me // 4 % 2, me // 2 % 2, me % 2
        self.index = fragment
        self.local = fragment_local[0]
        self.globs = jnp.swapaxes(global_params, 1, 2)
        self.outers = jnp.swapaxes(outer_moment, 1, 2)

    def swap_params(self, *since):
        own = chosen_params(*tie([self.globs, self.outers], *since), self.index)
        self.params = (own, swap_pair(own))

    def swap_cores(self, *since):
        mine, other = turn_fragment(tie([self.local], *since)[0], self.core)
        self.state = (mine, swap_core(other))

    def reduce_far(self, *since):
        mine, other = halve(*tie(self.state, *since), self.far, "halve_far")
        self.state = (mine, swap_far(other))

    def reduce_near(self, *since):
        mine, other = halve(*tie(self.state, *since), self.near, "halve_near")
        self.state = (mine[0], swap_near(other)[0])

    def reduce_pair(self, *since):
        mine = total(*tie(self.state, *since))
        self.state = (mine, swap_pair(mine))

    def gather_near(self, *since):
        mine, other = tie(self.state, *since)
        updated, self.new_global, self.new_outer = nesterov(
            mine,
            other,
            *self.params,
            self.globs,
            self.outers,
            self.index,
            self.pair,
            lax.axis_size("rep"),
        )
        updated = updated[None]
        self.state = (updated, swap_near(updated))

    def gather_far(self, *since):
        both = stack(*tie(self.state, *since), self.near, "stack_near")
        self.state = (both, swap_far(both))

    def gather_cores(self, *since):
        both = stack(*tie(self.state, *since), self.far, "stack_far")
        self.state = (both, swap_core(both))

    def results(self):
        return (
            weave(*self.state, self.core)[None],
            jnp.swapaxes(self.new_global, 1, 2),
            jnp.swapaxes(self.new_outer, 1, 2),
        )


def tie(values, *others):
    return lax.optimization_barrier((tuple(values), others))[0]


def body(
    tokens,
    targets,
    weight,
    moment_first,
    moment_second,
    fragment_local,
    global_params,
    outer_moment,
    fragment,
):
    outer = Outer(fragment_local, global_params, outer_moment, fragment)
    shard = weight[0]
    width = tokens.shape[1]
    inv_root = 1.0 / math.sqrt(width)
    scale = 1.0 / math.sqrt(tokens.shape[0] * lax.axis_size("fsdp"))

    owns = split_columns(shard, CHUNKS)
    blocks = [[own, along_z(own, -1), along_z(own, 1)] for own in owns]
    pieces = pack_tokens(tokens)
    far = {k: along_x(pieces[k], k) for k in (2, 1, 3)}
    pieces = [pieces[0], far[1], far[2], far[3]]
    def pass_on(block):
        own, following, previous = block
        top, bottom = outer_halves(previous, following)
        return [own, following, along_z(top, 1), along_z(bottom, -1), previous]

    def back(keys):
        return {k: along_x(keys[k], -k) for k in (2, 1, 3)}

    def out(keys, got, part):
        resid = residual(keys[0], [got[1], got[2], got[3]], targets, part, inv_root)
        there = {k: along_x(resid, k) for k in (2, 1, 3)}
        return [resid, there[1], there[2], there[3]]

    outer.swap_params(blocks[0][2])
    keys = partial_keys(pieces, pass_on(blocks[0]), HEAVY)
    got = back(keys)
    outer.swap_cores(keys[0])
    outer.reduce_far()
    block = pass_on(tie(blocks[1], got[1]))
    turned = transpose_tokens(tie(pieces, keys[0]))
    resids = out(keys, got, 0)
    outer.reduce_near()

    keys = partial_keys(pieces, tie(block, resids[0]), HEAVY)
    got = back(keys)
    outer.reduce_pair(*block)
    outer.gather_near()
    outer.gather_far()

    own, one, far_a, far_b, three = partial_grad(turned, resids)
    far_a, far_b = along_z(far_a, 1), along_z(far_b, -1)
    resids = out(keys, got, 1)

    up, down = add_halves(one, far_a, three, far_b)
    left, right = along_z(up, 1), along_z(down, -1)
    outer.gather_cores(up)

    own1, one1, far_a, far_b, three1 = partial_grad(turned, tie(resids, up))
    far_a, far_b = along_z(far_a, 1), along_z(far_b, -1)
    staged = load(tie([shard, moment_first[0], moment_second[0]], own1), "load_state")

    up, down = add_halves(one1, far_a, three1, far_b)
    left1, right1 = along_z(up, 1), along_z(down, -1)
    outs = adam_columns(0, CHUNKS, scale, own, left, right, *staged, None)
    outs = adam_columns(1, CHUNKS, scale, own1, left1, right1, *staged, outs)
    new_weight, new_first, new_second = outs
    return (new_weight[None], new_first[None], new_second[None], *outer.results())


def solution(mesh):
    return jax.shard_map(
        body,
        mesh=mesh,
        in_specs=(
            P(("rep", "fsdp"), None),
            P(("rep", "fsdp"), None),
            P("rep", "fsdp", None),
            P("rep", "fsdp", None),
            P("rep", "fsdp", None),
            P("rep", "fsdp", None),
            P(None, "fsdp", "rep"),
            P(None, "fsdp", "rep"),
            P(),
        ),
        out_specs=(
            P("rep", "fsdp", None),
            P("rep", "fsdp", None),
            P("rep", "fsdp", None),
            P("rep", "fsdp", None),
            P(None, "fsdp", "rep"),
            P(None, "fsdp", "rep"),
        ),
        check_vma=False,
    )
```

```python
import math

import jax
import jax.numpy as jnp
from jax import lax
from jax.experimental import pallas as pl
from jax.experimental.pallas import tpu as pltpu
from jax.sharding import PartitionSpec as P

CHUNKS = 2
NX = 4
NZ = 4
NY = 4
LIMIT = 16 * 2**20
LIGHT = pl.CostEstimate(flops=1, bytes_accessed=1, transcendentals=0)
HEAVY = pl.CostEstimate(flops=4 * 10**10, bytes_accessed=10**6, transcendentals=0)

f32 = jnp.float32
bf16 = jnp.bfloat16


def along_x(value, step):
    pairs = [(a * NX + b, a * NX + (b + step) % NX) for a in range(NZ) for b in range(NX)]
    return lax.ppermute(value, "fsdp", pairs)


def along_z(value, step):
    pairs = [(a * NX + b, (a + step) % NZ * NX + b) for a in range(NZ) for b in range(NX)]
    return lax.ppermute(value, "fsdp", pairs)


def swap_near(value):
    return lax.ppermute(value, "rep", [(r, r ^ 4) for r in range(16)])


def swap_far(value):
    return lax.ppermute(value, "rep", [(r, r ^ 8) for r in range(16)])


def swap_core(value):
    return lax.ppermute(value, "rep", [(r, r ^ 1) for r in range(16)])


def swap_pair(value):
    return lax.ppermute(value, "rep", [(r, r ^ 2) for r in range(16)])


def kernel_call(kernel, inputs, outs, cost, name, scratch=(), blocked=None, **options):
    blocked = blocked or {}
    specs = [
        blocked.get(n, pl.BlockSpec(memory_space=pltpu.VMEM)) for n in range(len(inputs))
    ]
    inputs = [
        value if n in blocked else pltpu.with_memory_space_constraint(value, pltpu.VMEM)
        for n, value in enumerate(inputs)
    ]
    return pl.pallas_call(
        kernel,
        in_specs=specs,
        out_specs=[pl.BlockSpec(memory_space=pltpu.VMEM)] * len(outs),
        out_shape=[pltpu.VMEM(shape, dtype) for shape, dtype in outs],
        scratch_shapes=list(scratch),
        compiler_params=pltpu.CompilerParams(vmem_limit_bytes=LIMIT),
        cost_estimate=cost,
        name=name,
        **options,
    )(*inputs)


SMALL = pl.BlockSpec(memory_space=pltpu.SMEM)
ANYWHERE = pl.BlockSpec(memory_space=pl.ANY)
IN_HBM = pl.BlockSpec(memory_space=pltpu.HBM)


def in_hbm(value):
    return pltpu.with_memory_space_constraint(value, pltpu.HBM)


def pack_tokens(tokens):
    rows, width = tokens.shape
    block = width // (NX * NZ)
    me = lax.axis_index("fsdp").astype(jnp.int32).reshape(1)

    def kernel(me_ref, source, *refs):
        sems = refs[-1]
        z, x = me_ref[0] // NX, me_ref[0] % NX
        copies = []
        for k in range(NX):
            for j in range(NZ):
                start = ((z + j) % NZ * NX + (x + k) % NX) * block
                copies.append(
                    pltpu.make_async_copy(
                        source.at[:, pl.ds(pl.multiple_of(start, 128), block)],
                        refs[k].at[:, j * block : (j + 1) * block],
                        sems.at[k, j],
                    )
                )
        for copy in copies:
            copy.start()
        for copy in copies:
            copy.wait()

    return kernel_call(
        kernel,
        [me, tokens],
        [((rows, NZ * block), tokens.dtype)] * NX,
        LIGHT,
        "pack_tokens",
        scratch=[pltpu.SemaphoreType.DMA((NX, NZ))],
        blocked={0: SMALL, 1: ANYWHERE},
    )


def load(arrays, name):
    count = len(arrays)

    def kernel(*refs):
        copies = [
            pltpu.make_async_copy(refs[n], refs[count + n], refs[-1].at[n]) for n in range(count)
        ]
        for copy in copies:
            copy.start()
        for copy in copies:
            copy.wait()

    return kernel_call(
        kernel,
        [in_hbm(array) for array in arrays],
        [(array.shape, array.dtype) for array in arrays],
        LIGHT,
        name,
        scratch=[pltpu.SemaphoreType.DMA((count,))],
        blocked={n: IN_HBM for n in range(count)},
    )


def transpose_tokens(pieces):
    rows, width = pieces[0].shape

    def kernel(*refs):
        out = refs[-1]
        for k in range(NX):
            out[:, k * rows : (k + 1) * rows] = refs[k][...].T

    return kernel_call(
        kernel, pieces, [((width, NX * rows), bf16)], HEAVY, "transpose_tokens"
    )[0]


def split_columns(value, parts):
    rows, width = value.shape
    columns = width // parts

    def kernel(source, *refs):
        copies = [
            pltpu.make_async_copy(
                source.at[:, c * columns : (c + 1) * columns], refs[c], refs[-1].at[c]
            )
            for c in range(parts)
        ]
        for copy in copies:
            copy.start()
        for copy in copies:
            copy.wait()

    return kernel_call(
        kernel,
        [value],
        [((rows, columns), value.dtype)] * parts,
        LIGHT,
        "split_columns",
        scratch=[pltpu.SemaphoreType.DMA((parts,))],
        blocked={0: ANYWHERE},
    )


def outer_halves(previous, following):
    half = previous.shape[0] // 2

    def kernel(previous, following, top, bottom):
        top[...] = previous[:half, :]
        bottom[...] = following[half:, :]

    return kernel_call(
        kernel, [previous, following], [((half, previous.shape[1]), bf16)] * 2, LIGHT, "outer_halves"
    )


def partial_keys(pieces, blocks, cost):
    rows, width = pieces[0].shape
    columns = blocks[0].shape[1]

    def kernel(*refs):
        tokens = refs[:NX]
        weights = refs[NX : NX + len(blocks)]
        outs = refs[NX + len(blocks) : -1]
        whole = refs[-1]
        at = 0
        for ref in weights:
            whole[at : at + ref.shape[0], :] = ref[...]
            at += ref.shape[0]
        for k in (2, 1, 3, 0):
            outs[k][...] = jnp.dot(
                tokens[k][...], whole[...], preferred_element_type=f32
            ).astype(outs[k].dtype)

    return kernel_call(
        kernel,
        [*pieces, *blocks],
        [((rows, columns), f32 if k == 0 else bf16) for k in range(NX)],
        cost,
        "partial_keys",
        scratch=[pltpu.VMEM((width, columns), bf16)],
    )


def residual(own, others, goals, part, inv_root):
    chosen = slice(part * own.shape[1], (part + 1) * own.shape[1])

    def kernel(own, one, two, three, goals, out):
        total = own[...] + one[...].astype(f32) + two[...].astype(f32) + three[...].astype(f32)
        out[...] = (total * inv_root - goals[:, chosen].astype(f32)).astype(bf16)

    return kernel_call(kernel, [own, *others, goals], [(own.shape, bf16)], LIGHT, "residual")[0]


def partial_grad(turned, resids):
    width, tokens = turned.shape
    rows, columns = resids[0].shape
    block = width // NZ
    half = block // 2

    def kernel(turned_ref, *refs):
        resid = refs[:NX]
        own, one, far_a, far_b, three, whole = refs[NX:]
        for k in range(NX):
            whole[k * rows : (k + 1) * rows, :] = resid[k][...]
        far = jnp.dot(
            turned_ref[2 * block : 3 * block, :], whole[...], preferred_element_type=f32
        )
        far_a[...] = far[:half].astype(bf16)
        far_b[...] = far[half:].astype(bf16)
        for j, out in ((1, one), (3, three), (0, own)):
            out[...] = jnp.dot(
                turned_ref[j * block : (j + 1) * block, :], whole[...], preferred_element_type=f32
            ).astype(out.dtype)

    return kernel_call(
        kernel,
        [turned, *resids],
        [
            ((block, columns), f32),
            ((block, columns), bf16),
            ((half, columns), bf16),
            ((half, columns), bf16),
            ((block, columns), bf16),
        ],
        HEAVY,
        "partial_grad",
        scratch=[pltpu.VMEM((tokens, columns), bf16)],
    )


def add_halves(one, far_a, three, far_b):
    half = far_a.shape[0]

    def kernel(one, far_a, three, far_b, up, down):
        up[:half, :] = (one[:half, :].astype(f32) + far_a[...].astype(f32)).astype(bf16)
        up[half:, :] = one[half:, :]
        down[:half, :] = three[:half, :]
        down[half:, :] = (three[half:, :].astype(f32) + far_b[...].astype(f32)).astype(bf16)

    return kernel_call(
        kernel, [one, far_a, three, far_b], [(one.shape, bf16)] * 2, LIGHT, "add_halves"
    )


def adam_columns(part, parts, scale, own, left, right, weight, first, second, earlier):
    rows, width = weight.shape
    columns = width // parts
    tiles = 3
    tile = rows // tiles
    chosen = slice(part * columns, (part + 1) * columns)

    def kernel(own, left, right, weight, first, second, *refs):
        new_weight, new_first, new_second = refs[-3:]
        at = pl.ds(pl.multiple_of(pl.program_id(0) * tile, tile), tile)
        grad = (own[at, :] + left[at, :].astype(f32) + right[at, :].astype(f32)) * scale
        moved = 0.9 * first[at, chosen] + 0.1 * grad
        spread = 0.95 * second[at, chosen] + 0.05 * grad * grad
        wide = weight[at, chosen].astype(f32)
        new_first[...] = moved
        new_second[...] = spread
        new_weight[...] = (wide - 0.3 * (moved / (jnp.sqrt(spread) + 1e-08) + 0.1 * wide)).astype(
            bf16
        )

    inputs = [own, left, right, weight, first, second]
    place = pl.BlockSpec((tile, columns), lambda i: (i, part))
    return pl.pallas_call(
        kernel,
        grid=(tiles,),
        in_specs=[pl.BlockSpec(memory_space=pltpu.VMEM)] * 6
        + [ANYWHERE] * (3 if earlier else 0),
        out_specs=[place] * 3,
        out_shape=[
            jax.ShapeDtypeStruct((rows, width), bf16),
            jax.ShapeDtypeStruct((rows, width), f32),
            jax.ShapeDtypeStruct((rows, width), f32),
        ],
        input_output_aliases={6 + n: n for n in range(3)} if earlier else {},
        compiler_params=pltpu.CompilerParams(vmem_limit_bytes=LIMIT),
        cost_estimate=LIGHT,
        name="adam_columns",
    )(*[pltpu.with_memory_space_constraint(value, pltpu.VMEM) for value in inputs], *(earlier or ()))


def turn_fragment(fragment, core):
    rows, width = fragment.shape
    columns = width // 16

    def kernel(core_ref, source, mine, other):
        low = core_ref[0] == 0
        for y in range(NY):
            for pair in range(2):
                at = (y * 2 + pair) * 2 * columns
                both = source[:, at : at + 2 * columns].T
                mine[y, pair] = jnp.where(low, both[:columns], both[columns:])
                other[y, pair] = jnp.where(low, both[columns:], both[:columns])

    return kernel_call(
        kernel,
        [core, fragment],
        [((NY, 2, columns, rows), bf16)] * 2,
        LIGHT,
        "turn_fragment",
        blocked={0: SMALL},
    )


def halve(mine, other, keep, kind, name):
    shape = (mine.shape[0] // 2, *mine.shape[1:])

    def kernel(keep_ref, mine, other, kept, sent):
        for out, which in ((sent, 1 - keep_ref[0]), (kept, keep_ref[0])):
            at = pl.ds(which * shape[0], shape[0])
            out[...] = (mine[at].astype(f32) + other[at].astype(f32)).astype(out.dtype)

    return kernel_call(
        kernel,
        [keep, mine, other],
        [(shape, f32), (shape, kind)],
        LIGHT,
        name,
        blocked={0: SMALL},
    )


def total(mine, other):
    def kernel(mine, other, out):
        out[...] = mine[...] + other[...]

    return kernel_call(kernel, [mine, other], [(mine.shape, f32)], LIGHT, "total")[0]


def stack(mine, other, second, name):
    count = mine.shape[0]

    def kernel(second_ref, mine, other, out):
        out[pl.ds(second_ref[0] * count, count)] = mine[...]
        out[pl.ds((1 - second_ref[0]) * count, count)] = other[...]

    return kernel_call(
        kernel,
        [second, mine, other],
        [((2 * count, *mine.shape[1:]), mine.dtype)],
        LIGHT,
        name,
        blocked={0: SMALL},
    )[0]


def chosen_params(globs, outers, index):
    def kernel(index_ref, globs, outers, out):
        out[0] = globs[index_ref[0]]
        out[1] = outers[index_ref[0]]

    return kernel_call(
        kernel,
        [index, globs, outers],
        [((2, *globs.shape[1:]), f32)],
        LIGHT,
        "chosen_params",
        blocked={0: SMALL},
    )[0]


def nesterov(mine, other, own, theirs, globs, outers, index, pair, replicas):
    frags = globs.shape[0]

    def kernel(index_ref, pair_ref, mine, other, own, theirs, globs, outers, *outs):
        updated, new_global, new_outer = outs
        new_global[...] = globs[...]
        new_outer[...] = outers[...]
        for which, params in ((pair_ref[0], own), (1 - pair_ref[0], theirs)):
            mean_local = (mine[which] + other[which]) / replicas
            glob = params[0]
            moment = 0.9 * params[1] + (glob - mean_local)
            after = glob - 0.7 * (glob - mean_local + 0.9 * moment)
            updated[which] = after.astype(bf16)
            if params is own:
                new_global[index_ref[0]] = after
                new_outer[index_ref[0]] = moment

    return pl.pallas_call(
        kernel,
        in_specs=[SMALL] * 2 + [pl.BlockSpec(memory_space=pltpu.VMEM)] * 6,
        out_specs=[pl.BlockSpec(memory_space=pltpu.VMEM)] + [pl.BlockSpec()] * 2,
        out_shape=[
            pltpu.VMEM(mine.shape, bf16),
            jax.ShapeDtypeStruct(globs.shape, f32),
            jax.ShapeDtypeStruct(globs.shape, f32),
        ],
        compiler_params=pltpu.CompilerParams(vmem_limit_bytes=LIMIT),
        cost_estimate=LIGHT,
        name="nesterov",
    )(
        index,
        pair,
        *[
            pltpu.with_memory_space_constraint(value, pltpu.VMEM)
            for value in (mine, other, own, theirs, globs, outers)
        ],
    )


def weave(mine, other, core):
    ys, pairs, columns, rows = mine.shape

    def kernel(core_ref, mine, other, out):
        low = core_ref[0] == 0
        for y in range(ys):
            for pair in range(pairs):
                a, b = mine[y, pair], other[y, pair]
                both = jnp.concatenate([jnp.where(low, a, b), jnp.where(low, b, a)])
                at = (y * pairs + pair) * 2 * columns
                out[:, at : at + 2 * columns] = both.T

    return pl.pallas_call(
        kernel,
        in_specs=[SMALL] + [pl.BlockSpec(memory_space=pltpu.VMEM)] * 2,
        out_shape=jax.ShapeDtypeStruct((rows, 2 * columns * ys * pairs), bf16),
        compiler_params=pltpu.CompilerParams(vmem_limit_bytes=LIMIT),
        cost_estimate=LIGHT,
        name="weave",
    )(core, *[pltpu.with_memory_space_constraint(v, pltpu.VMEM) for v in (mine, other)])


class Outer:
    def __init__(self, fragment_local, global_params, outer_moment, fragment):
        me = lax.axis_index("rep").astype(jnp.int32).reshape(1)
        self.far, self.near, self.pair, self.core = me // 8, me // 4 % 2, me // 2 % 2, me % 2
        self.index = fragment
        self.local = fragment_local[0]
        self.globs = jnp.swapaxes(global_params, 1, 2)
        self.outers = jnp.swapaxes(outer_moment, 1, 2)

    def swap_params(self, *since):
        own = chosen_params(*tie([self.globs, self.outers], *since), self.index)
        self.params = (own, swap_pair(own))

    def swap_cores(self, *since):
        mine, other = turn_fragment(tie([self.local], *since)[0], self.core)
        self.state = (mine, swap_core(other))

    def reduce_far(self, *since):
        mine, other = halve(*tie(self.state, *since), self.far, bf16, "halve_far")
        self.state = (mine, swap_far(other))

    def reduce_near(self, *since):
        mine, other = halve(*tie(self.state, *since), self.near, f32, "halve_near")
        self.state = (mine[0], swap_near(other)[0])

    def reduce_pair(self, *since):
        mine = total(*tie(self.state, *since))
        self.state = (mine, swap_pair(mine))

    def gather_near(self, *since):
        mine, other = tie(self.state, *since)
        updated, self.new_global, self.new_outer = nesterov(
            mine,
            other,
            *self.params,
            self.globs,
            self.outers,
            self.index,
            self.pair,
            lax.axis_size("rep"),
        )
        updated = updated[None]
        self.state = (updated, swap_near(updated))

    def gather_far(self, *since):
        both = stack(*tie(self.state, *since), self.near, "stack_near")
        self.state = (both, swap_far(both))

    def gather_cores(self, *since):
        both = stack(*tie(self.state, *since), self.far, "stack_far")
        self.state = (both, swap_core(both))

    def results(self):
        return (
            weave(*self.state, self.core)[None],
            jnp.swapaxes(self.new_global, 1, 2),
            jnp.swapaxes(self.new_outer, 1, 2),
        )


def tie(values, *others):
    return lax.optimization_barrier((tuple(values), others))[0]


def body(
    tokens,
    targets,
    weight,
    moment_first,
    moment_second,
    fragment_local,
    global_params,
    outer_moment,
    fragment,
):
    outer = Outer(fragment_local, global_params, outer_moment, fragment)
    shard = weight[0]
    width = tokens.shape[1]
    inv_root = 1.0 / math.sqrt(width)
    scale = 1.0 / math.sqrt(tokens.shape[0] * lax.axis_size("fsdp"))

    owns = split_columns(shard, CHUNKS)
    blocks = [[own, along_z(own, -1), along_z(own, 1)] for own in owns]
    pieces = pack_tokens(tokens)
    far = {k: along_x(pieces[k], k) for k in (2, 1, 3)}
    pieces = [pieces[0], far[1], far[2], far[3]]
    def pass_on(block):
        own, following, previous = block
        top, bottom = outer_halves(previous, following)
        return [own, following, along_z(top, 1), along_z(bottom, -1), previous]

    def back(keys):
        return {k: along_x(keys[k], -k) for k in (2, 1, 3)}

    def out(keys, got, part):
        resid = residual(keys[0], [got[1], got[2], got[3]], targets, part, inv_root)
        there = {k: along_x(resid, k) for k in (2, 1, 3)}
        return [resid, there[1], there[2], there[3]]

    outer.swap_params(blocks[0][2])
    keys = partial_keys(pieces, pass_on(blocks[0]), HEAVY)
    got = back(keys)
    outer.swap_cores(keys[0])
    outer.reduce_far()
    block = pass_on(tie(blocks[1], got[1]))
    turned = transpose_tokens(tie(pieces, keys[0]))
    resids = out(keys, got, 0)
    outer.reduce_near()

    keys = partial_keys(pieces, tie(block, resids[0]), HEAVY)
    got = back(keys)
    outer.reduce_pair(*block)
    outer.gather_near()
    outer.gather_far()

    own, one, far_a, far_b, three = partial_grad(turned, resids)
    far_a, far_b = along_z(far_a, 1), along_z(far_b, -1)
    resids = out(keys, got, 1)

    up, down = add_halves(one, far_a, three, far_b)
    left, right = along_z(up, 1), along_z(down, -1)
    outer.gather_cores(up)

    own1, one1, far_a, far_b, three1 = partial_grad(turned, tie(resids, far_a))
    far_a, far_b = along_z(far_a, 1), along_z(far_b, -1)
    staged = load(tie([shard, moment_first[0], moment_second[0]], own1), "load_state")

    up, down = add_halves(one1, far_a, three1, far_b)
    left1, right1 = along_z(up, 1), along_z(down, -1)
    outs = adam_columns(0, CHUNKS, scale, own, left, right, *staged, None)
    outs = adam_columns(1, CHUNKS, scale, own1, left1, right1, *staged, outs)
    new_weight, new_first, new_second = outs
    return (new_weight[None], new_first[None], new_second[None], *outer.results())


def solution(mesh):
    return jax.shard_map(
        body,
        mesh=mesh,
        in_specs=(
            P(("rep", "fsdp"), None),
            P(("rep", "fsdp"), None),
            P("rep", "fsdp", None),
            P("rep", "fsdp", None),
            P("rep", "fsdp", None),
            P("rep", "fsdp", None),
            P(None, "fsdp", "rep"),
            P(None, "fsdp", "rep"),
            P(),
        ),
        out_specs=(
            P("rep", "fsdp", None),
            P("rep", "fsdp", None),
            P("rep", "fsdp", None),
            P("rep", "fsdp", None),
            P(None, "fsdp", "rep"),
            P(None, "fsdp", "rep"),
        ),
        check_vma=False,
    )
```
